256 devices in a mesh: coils: 8 (over y, x_hi), slabs: 32 (over z, x_lo, core).
Axes of the slice: x: 4 (x_hi: 2, x_lo: 2; x = x_hi * 2 + x_lo), y: 4, z: 8, core: 2. Of those that a mesh axis runs over, the one named last changes fastest.
Arguments:
- kspace: float32 [2, 16, 96, 128, 256], P(None, 'coils', None, 'slabs'), may hold values from -6 to 6
- measured: float32 [2, 16, 24, 128, 256], P(None, 'coils', None, 'slabs'), may hold values from -6 to 6
- sampled_lines: int32 [24], replicated, may hold values from 0 to 95, as said below
- coil_maps: float32 [2, 16, 96, 128, 256], P(None, 'coils', 'slabs'), may hold values from -1.5 to 1.5
- step_size: float32 [1], replicated, may hold values from 0.5 to 2
- conv_one: bfloat16 [3, 3, 3, 18, 2], replicated, may hold values from -0.875 to 0.875
- bias_one: float32 [18], replicated, may hold values from -3 to 3
- conv_two: bfloat16 [3, 3, 3, 2, 18], replicated, may hold values from -0.25 to 0.25
- bias_two: float32 [2], replicated, may hold values from -3 to 3
- cotangent: float32 [2, 16, 96, 128, 256], P(None, 'coils', None, 'slabs'), may hold values from -0.006 to 0.006
Outputs:
- next_kspace: float32 [2, 16, 96, 128, 256], P(None, 'coils', None, 'slabs')
- grad_conv_one: float32 [3, 3, 3, 18, 2], replicated
- grad_bias_one: float32 [18], replicated
- grad_conv_two: float32 [3, 3, 3, 2, 18], replicated
- grad_bias_two: float32 [2], replicated
The draws below stay inside these ranges and needn't reach their ends.
Inputs may be any that keep to these rules, and one draw needn't show every extreme that they name: `sampled_lines`: 24 distinct slice-encode positions; 0, 1, 94 and 95 are always among them.
All inputs are finite; a program needn't handle non-finite values.
Results may differ from the reference program's by a relative error of at most 0.0057.
Values may be sent and summed in bfloat16 or wider, within the bound.
A program may use at most 320 MiB of HBM per device.

```python
import math
import jax
import jax.numpy as jnp
from jax import lax

NS = 96
NP = 128
NR = 256
CH = 18
COILS = 16
LINES = 24


def draw_sampled_lines(key, part):
    key = jax.random.fold_in(key, 11)
    middle = jax.random.permutation(key, NS - 4)[:LINES - 4].astype(jnp.int32) + 2
    edges = jnp.array([0, 1, NS - 2, NS - 1], dtype=jnp.int32)
    return jnp.concatenate([edges, middle])


def block_scale(own_key, shape, pieces, least, top_value):
    level = 1.0
    for position, blocks in pieces:
        heights = jax.random.uniform(jax.random.fold_in(jax.random.fold_in(own_key, 6), position), (blocks,), jnp.float32, least / len(pieces), top_value / len(pieces))
        level = level * jnp.repeat(jnp.exp(heights), shape[position] // blocks).reshape((-1,) + (1,) * (len(shape) - 1 - position))
    return level


def noise(own_key, shape, scale, bound, pieces=(), held_as=jnp.bfloat16):
    drawn = scale * jax.random.normal(own_key, shape, jnp.float32)
    if pieces:
        drawn = drawn * block_scale(own_key, shape, pieces, -0.22, 0.18)
    return jnp.clip(drawn, -bound, bound).astype(held_as)


def setup_inputs(seed: int = 0) -> dict:
    seeds = jax.random.split(jax.random.key(seed), 11)
    kspace = noise(seeds[0], (2, COILS, NS, NP, NR), 1.0, 6.0, ((1, 8), (3, 32)), jnp.float32)
    measured = noise(seeds[1], (2, COILS, LINES, NP, NR), 1.0, 6.0, ((1, 8), (3, 32)), jnp.float32)
    sampled_lines = draw_sampled_lines(jax.random.fold_in(seeds[10], 71), 0)
    coil_maps = noise(seeds[3], (2, COILS, NS, NP, NR), COILS ** -0.5, 1.5, ((1, 8), (2, 32)), jnp.float32)
    step_size = jnp.clip(jnp.exp(jax.random.uniform(seeds[4], (1,), jnp.float32, math.log(0.5), math.log(2.0))), 0.5, 2.0)
    conv_one = noise(seeds[5], (3, 3, 3, CH, 2), 54 ** -0.5, 0.875)
    bias_one = noise(seeds[6], (CH,), 0.5, 3.0, (), jnp.float32)
    conv_two = noise(seeds[7], (3, 3, 3, 2, CH), (27 * CH) ** -0.5, 0.25)
    bias_two = noise(seeds[8], (2,), 0.5, 3.0, (), jnp.float32)
    cotangent = noise(seeds[9], (2, COILS, NS, NP, NR), 0.001, 0.006, ((1, 8), (3, 32)), jnp.float32)
    return dict(kspace=kspace, measured=measured, sampled_lines=sampled_lines, coil_maps=coil_maps, step_size=step_size, conv_one=conv_one, bias_one=bias_one, conv_two=conv_two, bias_two=bias_two, cotangent=cotangent)


def rounded(values):
    return lax.optimization_barrier(values.astype(jnp.bfloat16))


def pad_grid(values):
    return jnp.pad(values, ((0, 0), (1, 1), (1, 1), (1, 1)))


def tap_slice(padded_values, offset, extent, flip):
    shift_one = offset // 9
    shift_two = (offset // 3) % 3
    shift_three = offset % 3
    if flip:
        shift_one = 2 - shift_one
        shift_two = 2 - shift_two
        shift_three = 2 - shift_three
    return padded_values[:, shift_one:shift_one + extent[0], shift_two:shift_two + extent[1], shift_three:shift_three + extent[2]]


def coil_combine(spectra_pair, sensitivity):
    spectra = lax.complex(spectra_pair[0], spectra_pair[1])
    images = jnp.fft.ifftn(spectra, axes=(1, 2, 3), norm="ortho")
    combined = jnp.sum(jnp.conj(sensitivity) * images, axis=0)
    return jnp.stack([jnp.real(combined), jnp.imag(combined)]).astype(jnp.float32)


def reference(kspace, measured, sampled_lines, coil_maps, step_size, conv_one, bias_one, conv_two, bias_two, cotangent):
    sensitivity = lax.complex(coil_maps[0], coil_maps[1])
    image_field = coil_combine(kspace, sensitivity)
    extent = image_field.shape[1:]
    image_pad = pad_grid(rounded(image_field)).astype(jnp.float32)
    taps_one = conv_one.reshape(27, CH, 2).astype(jnp.float32)
    taps_two = conv_two.reshape(27, 2, CH).astype(jnp.float32)
    pre_one = jnp.zeros((CH,) + extent, jnp.float32) + bias_one[:, None, None, None]
    for offset in range(27):
        pre_one = pre_one + jnp.einsum("oc,cspr->ospr", taps_one[offset], tap_slice(image_pad, offset, extent, False), precision=lax.Precision.HIGHEST)
    hidden_low = rounded(jax.nn.silu(pre_one))
    hidden_pad = pad_grid(hidden_low).astype(jnp.float32)
    update = jnp.zeros((2,) + extent, jnp.float32) + bias_two[:, None, None, None]
    for offset in range(27):
        update = update + jnp.einsum("oc,cspr->ospr", taps_two[offset], tap_slice(hidden_pad, offset, extent, False), precision=lax.Precision.HIGHEST)
    update_complex = lax.complex(update[0], update[1])
    regularized = jnp.fft.fftn(sensitivity * update_complex[None], axes=(1, 2, 3), norm="ortho")
    spectra = lax.complex(kspace[0], kspace[1])
    measured_complex = lax.complex(measured[0], measured[1])
    misfit = spectra[:, sampled_lines] - measured_complex
    spread = jnp.zeros_like(spectra).at[:, sampled_lines].add(misfit)
    next_complex = spectra - step_size[0] * spread + regularized
    next_kspace = jnp.stack([jnp.real(next_complex), jnp.imag(next_complex)]).astype(jnp.float32)

    gradient_field = coil_combine(cotangent, sensitivity)
    grad_bias_two = jnp.sum(gradient_field, axis=(1, 2, 3))
    grad_pad = pad_grid(rounded(gradient_field)).astype(jnp.float32)
    hidden_wide = hidden_low.astype(jnp.float32)
    back_hidden = jnp.zeros((CH,) + extent, jnp.float32)
    taps_grad_two = []
    for offset in range(27):
        shifted = tap_slice(grad_pad, offset, extent, True)
        taps_grad_two.append(jnp.einsum("ospr,cspr->oc", shifted, hidden_wide, precision=lax.Precision.HIGHEST))
        back_hidden = back_hidden + jnp.einsum("oc,ospr->cspr", taps_two[offset], shifted, precision=lax.Precision.HIGHEST)
    sigmoid_pre = jax.nn.sigmoid(pre_one)
    back_pre = back_hidden * sigmoid_pre * (1.0 + pre_one * (1.0 - sigmoid_pre))
    grad_bias_one = jnp.sum(back_pre, axis=(1, 2, 3))
    back_wide = rounded(back_pre).astype(jnp.float32)
    taps_grad_one = []
    for offset in range(27):
        taps_grad_one.append(jnp.einsum("ospr,cspr->oc", back_wide, tap_slice(image_pad, offset, extent, False), precision=lax.Precision.HIGHEST))
    grad_conv_one = jnp.stack(taps_grad_one).reshape(3, 3, 3, CH, 2)
    grad_conv_two = jnp.stack(taps_grad_two).reshape(3, 3, 3, 2, CH)
    return next_kspace, grad_conv_one, grad_bias_one, grad_conv_two, grad_bias_two
```

```python
from types import SimpleNamespace

import jax
import jax.numpy as jnp
import ml_dtypes
import numpy as np
from jax import lax
from jax.experimental import pallas as pl
from jax.experimental.pallas import tpu as pltpu
from jax.sharding import PartitionSpec as P

NS, NP, NR, CH, LINES = 96, 128, 256, 18, 24
BF, F32 = jnp.bfloat16, jnp.float32
MESH = pl.DeviceIdType.MESH


def dft(n, direction):
    index = np.arange(n)
    angles = (np.outer(index, index) % n) * (2.0 * np.pi / n)
    return np.cos(angles) / np.sqrt(n), direction * np.sin(angles) / np.sqrt(n)


def split_np(table):
    high = table.astype(ml_dtypes.bfloat16)
    low = (table - high.astype(np.float64)).astype(ml_dtypes.bfloat16)
    return high, low


def readout_table(direction, passes):
    cos, sin = dft(NR, direction)
    high, low = split_np(np.concatenate([cos, sin], axis=1))
    return np.concatenate([high, high, low] if passes == 3 else [high, low], axis=0)


def slice_table(direction):
    cos, sin = dft(NS, direction)
    high, low = split_np(np.block([[cos, -sin], [sin, cos]]))
    return np.concatenate([high, high, low, np.zeros((192, 64))], axis=1)


def phase_table(direction):
    cos, sin = dft(NP, direction)
    pair = np.array([[cos, -sin], [sin, cos]])
    full = np.zeros((2, 2, NP, 2, 2, NP))
    for c in range(2):
        full[c, :, :, c] = pair.transpose(0, 2, 1, 3)
    return full


def phase_inverse():
    full = phase_table(1.0).reshape(512, 2, 2, 32, 4)
    ordered = full.transpose(0, 3, 1, 2, 4).reshape(512, 512)
    return np.concatenate(split_np(ordered), axis=1)


def phase_forward():
    full = phase_table(-1.0).reshape(2, 2, 32, 4, 512)
    ordered = full.transpose(2, 0, 1, 3, 4).reshape(512, 512)
    high, low = split_np(ordered)
    return np.concatenate([high, high, low], axis=1)


def edge_picks():
    pick = np.zeros((2, 16, 8, 16), np.float32)
    for plane in range(6):
        for k in range(2):
            pick[0, plane * 2 + k, plane, k] = 1
            pick[1, plane * 2 + k, plane, 14 + k] = 1
    return pick.reshape(32, 128)


def window_picks(planes):
    count = len(planes)
    rows = count * 32
    pick = np.zeros((count, 2, 24, 128), np.float32)
    for i, plane in enumerate(planes):
        for part in range(2):
            for t in range(2):
                pick[i, part, t, rows + (plane * 2 + part) * 2 + t] = 1
                pick[i, part, 18 + t, rows + 16 + (plane * 2 + part) * 2 + t] = 1
            for t in range(16):
                pick[i, part, 2 + t, (i * 2 + part) * 16 + t] = 1
    return pick.reshape(count * 48, 128)


def constants():
    rows = np.arange(432)
    col_p = rows % 24
    row_p = rows // 24
    band = np.full((432, 512), -100.0)
    band[:, :432] = col_p[None, :] - row_p[:, None]
    row_pick = np.zeros((432, 128), np.float32)
    row_pick[rows, rows % 24] = 1
    row_pick_t = np.zeros((32, 512), np.float32)
    row_pick_t[rows % 24, rows] = 1
    col_pick = np.zeros((128, 512), np.float32)
    col_pick[rows // 24, rows] = 1
    out_rows = np.arange(96)
    band_two = np.full((96, 512), -100.0)
    band_two[:, :432] = row_p[None, :] - (out_rows % 16)[:, None]
    out_pair = out_rows // 16
    pick_two = np.zeros((9, 96, 128), np.float32)
    pick_one = np.zeros((3, 128, 512), np.float32)
    pick_back = np.zeros((3, 128, 512), np.float32)
    group = rows // 24
    g_ds, g_dr, g_part = group // 6, group // 2 % 3, group % 2
    for at in range(9):
        pick_two[at, out_rows, 54 + (at * 3 + out_pair // 2) * 2 + out_pair % 2] = 1
    for dp in range(3):
        pick_one[dp, (g_ds * 9 + dp * 3 + g_dr) * 2 + g_part, rows] = 1
        flipped = ((2 - g_ds) * 9 + (2 - dp) * 3 + 2 - g_dr) * 2 + g_part
        pick_back[dp, 54 + flipped, rows] = 1
    col_pick_two = np.zeros((128, 512), np.float32)
    col_pick_two[rows % 24, rows] = 1
    staged = dict(
        rtab_inv=readout_table(1.0, 3),
        stab_inv=slice_table(1.0),
        ptab_inv=phase_inverse(),
        ptab_fwd=phase_forward(),
        rtab_fwd=readout_table(-1.0, 2),
        stab_fwd=slice_table(-1.0),
        band=band,
        pick_one=pick_one,
        pick_back=pick_back,
        pick_two=pick_two,
    )
    direct = dict(
        pick_edge=edge_picks(),
        pick_prev=window_picks((1, 2)),
        pick_own=window_picks((0, 1, 2)),
        pick_next=window_picks((0, 1)),
        row_pick=row_pick,
        band_two=band_two,
        col_pick_two=col_pick_two,
        row_pick_t=row_pick_t,
        col_pick_t=col_pick.T,
    )

    def low(table):
        return {k: jnp.asarray(np.asarray(v).astype(ml_dtypes.bfloat16)) for k, v in table.items()}

    return low(staged), low(direct)


def dot(a, b):
    return lax.dot_general(a, b, (((1,), (0,)), ((), ())), preferred_element_type=F32)


def dot_rows(a, b):
    return lax.dot_general(a, b, (((1,), (1,)), ((), ())), preferred_element_type=F32)


def split(value):
    high = value.astype(BF)
    return high, (value - high.astype(F32)).astype(BF)


def thirds(value):
    high, rest = value.astype(BF), value
    rest = rest - high.astype(F32)
    middle = rest.astype(BF)
    return high, middle, (rest - middle.astype(F32)).astype(BF)


def pick_rows(pick, value):
    return sum(dot(pick, piece) for piece in thirds(value))


def pick_cols(value, pick):
    return sum(dot(piece, pick) for piece in thirds(value))


def blank(rows, lanes=256):
    return jnp.zeros((rows, lanes), BF)


def deep(value, rows=512):
    return jnp.concatenate([value, blank(rows - value.shape[0], value.shape[1])], axis=0)


def with_ones(value):
    return jnp.concatenate([value, jnp.ones((80, 256), BF)], axis=0)


def low_half(shape, axis):
    return lax.broadcasted_iota(jnp.int32, shape, axis) < 4


def to_rows(even, odd):
    first = low_half(even.shape, 1)
    low = jnp.where(first, even, pltpu.roll(odd, 4, 1))
    high = jnp.where(first, pltpu.roll(even, 4, 1), odd)
    return low.reshape(-1, 128), high.reshape(-1, 128)


def from_rows(low, high):
    low = low.reshape(-1, 8, 128)
    high = high.reshape(-1, 8, 128)
    first = low_half(low.shape, 1)
    even = jnp.where(first, low, pltpu.roll(high, 4, 1))
    odd = jnp.where(first, pltpu.roll(low, 4, 1), high)
    return even, odd


def kernel(h, s, out_ref, one_ref, bias_one_ref, two_ref, bias_two_ref):
    coil = lax.axis_index("coils")
    slab = lax.axis_index("slabs")

    load = SimpleNamespace()
    for at, (name, source) in enumerate(vars(h).items()):
        copy = pltpu.make_async_copy(source, getattr(s.stage, name), s.load_sem.at[at])
        setattr(load, name, copy)
        copy.start()

    barrier = pltpu.get_barrier_semaphore()

    def greet(target_coil, target_slab):
        pl.semaphore_signal(
            barrier, inc=1, device_id=(target_coil, target_slab), device_id_type=MESH
        )

    @pl.loop(1, 32)
    def _(k):
        greet(coil, lax.rem(slab + k, 32))

    @pl.loop(1, 8)
    def _(k):
        greet(lax.rem(coil + k, 8), slab)

    @pl.loop(1, 8)
    def _(k):
        greet(lax.rem(coil + k, 8), slab + 1 - 2 * lax.rem(slab, 2))

    for dc in (1, 7):
        for ds in (1, 31):
            greet(lax.rem(coil + dc, 8), lax.rem(slab + ds, 32))

    def to_send(v, send, keep):
        rtab = s.stage.rtab_inv[...]
        stab = s.stage.stab_inv[...]
        z, y = s.z, s.y
        for c in range(2):
            uv = []
            for part in range(2):
                low, high = to_rows(v[part, c, :, 0], v[part, c, :, 1])
                if keep:
                    s.rows[0, part, c] = low
                    s.rows[1, part, c] = high
                x_high, x_low = split(jnp.concatenate([low, high], axis=1))
                uv.append(dot(jnp.concatenate([x_high, x_low, x_high], axis=1), rtab))
            z_real = uv[0][:, :256] - uv[1][:, 256:]
            z_imag = uv[1][:, :256] + uv[0][:, 256:]
            for half in range(2):
                lanes = slice(half * 128, half * 128 + 128)
                z[half, 0, c] = z_real[:, lanes]
                z[half, 1, c] = z_imag[:, lanes]
            for p in range(4):
                pick = pl.ds(p, 96, stride=4)
                parts = [
                    jnp.concatenate([z[0, part, c, pick, :], z[1, part, c, pick, :]], axis=1)
                    for part in range(2)
                ]
                z_high, z_low = split(jnp.concatenate(parts, axis=0))
                out = dot(stab, deep(jnp.concatenate([z_high, z_low, z_high], axis=0), 640))
                for part in range(2):
                    for half in range(2):
                        y[half, pl.ds(c * 8 + part * 4 + p, 96, stride=16), :] = out[
                            part * 96 : part * 96 + 96, half * 128 : half * 128 + 128
                        ]
        full = jnp.concatenate([y[0], y[1]], axis=1).astype(BF)
        send[...] = full.reshape(32, 48, 256)

    def exchange(send, recv, send_sem, recv_sem, first, last):
        @pl.loop(first, last)
        def _(k):
            target = lax.rem(slab + lax.rem(k * 13, 32), 32)
            pltpu.make_async_remote_copy(
                src_ref=send.at[target],
                dst_ref=recv.at[slab],
                send_sem=send_sem,
                recv_sem=recv_sem,
                device_id=(coil, target),
                device_id_type=MESH,
            ).start()

    def drained(ref, sem):
        pltpu.make_async_copy(ref, ref, sem).wait()

    def exchange_sent(send, send_sem):
        drained(send.at[pl.ds(0, 31)], send_sem)

    def exchange_arrived(recv, recv_sem):
        drained(recv.at[pl.ds(0, 31)], recv_sem)

    def combine(recv, part_own, rs_send, rs_recv, send_sem, recv_sem, low):
        table = s.stage.ptab_inv[...]
        maps = s.stage.maps
        for plane in range(3):
            values = recv[:, 16 * plane : 16 * plane + 16, :].reshape(512, 256)
            image = dot(table, jnp.concatenate([values, values], axis=0))
            real = jnp.zeros((128, 256), F32)
            imag = jnp.zeros((128, 256), F32)
            for c in range(2):
                m_real, m_imag = maps[0, c, plane], maps[1, c, plane]
                i_real = image[c * 256 : c * 256 + 128]
                i_imag = image[c * 256 + 128 : c * 256 + 256]
                real = real + m_real * i_real + m_imag * i_imag
                imag = imag + m_real * i_imag - m_imag * i_real
            part_own[:, plane, 0] = real.reshape(8, 16, 256)
            part_own[:, plane, 1] = imag.reshape(8, 16, 256)
            if low:
                rs_send[:, plane, 0] = real.astype(BF).reshape(8, 16, 256)
                rs_send[:, plane, 1] = imag.astype(BF).reshape(8, 16, 256)

        @pl.loop(1, 8)
        def _(k):
            target = lax.rem(coil + k, 8)
            pltpu.make_async_remote_copy(
                src_ref=rs_send.at[target],
                dst_ref=rs_recv.at[coil],
                send_sem=send_sem,
                recv_sem=recv_sem,
                device_id=(target, slab),
                device_id_type=MESH,
            ).start()

        rs_recv[coil] = jnp.zeros((3, 2, 16, 256), rs_recv.dtype)

    def combined(part_own, rs_send, rs_recv, send_sem, recv_sem):
        drained(rs_recv.at[pl.ds(0, 7)], recv_sem)
        drained(rs_send.at[pl.ds(0, 7)], send_sem)
        total = part_own[coil]
        for k in range(8):
            total = total + rs_recv[k].astype(F32)
        return total

    def halo_start(field, planes, edges, hp_recv, he_recv, sems):
        planes[...] = field.astype(BF).reshape(3, 32, 256)
        picked = dot(s.pick_edge[...], deep(planes[...].reshape(96, 256), 128))
        edges[...] = picked.astype(BF).reshape(2, 16, 256)
        prev, after = lax.rem(slab + 31, 32), lax.rem(slab + 1, 32)

        def send(src, dst, pair, target):
            pltpu.make_async_remote_copy(
                src_ref=src, dst_ref=dst, send_sem=sems.at[pair], recv_sem=sems.at[pair + 1],
                device_id=target, device_id_type=MESH,
            ).start()

        send(planes.at[pl.ds(1, 2)], hp_recv.at[0], 0, (coil, after))
        send(planes.at[pl.ds(0, 2)], hp_recv.at[1], 0, (coil, prev))
        for at, target_slab in ((2, prev), (1, slab), (0, after)):
            send(edges.at[1], he_recv.at[at, 0], 2, (lax.rem(coil + 1, 8), target_slab))
            send(edges.at[0], he_recv.at[at, 1], 2, (lax.rem(coil + 7, 8), target_slab))

    def halo_finish(planes, hp_recv, he_recv, sems, x):
        drained(hp_recv, sems.at[1])
        drained(he_recv, sems.at[3])
        drained(hp_recv, sems.at[0])
        drained(he_recv, sems.at[2])
        zero_edge = jnp.zeros((16, 256), BF)

        def group(body, at):
            lower = jnp.where(coil > 0, he_recv[at, 0], zero_edge)
            upper = jnp.where(coil < 7, he_recv[at, 1], zero_edge)
            return jnp.concatenate([body, lower, upper], axis=0)

        before = group(hp_recv[0].reshape(64, 256), 0)
        own = group(planes[...].reshape(96, 256), 1)
        after = group(hp_recv[1].reshape(64, 256), 2)
        before = dot(s.pick_prev[...], deep(before, 128))
        after = dot(s.pick_next[...], deep(after, 128))
        before = jnp.where(slab > 0, before, jnp.zeros_like(before))
        after = jnp.where(slab < 31, after, jnp.zeros_like(after))
        window = jnp.concatenate([before, dot(s.pick_own[...], own), after], axis=0)
        lane = lax.broadcasted_iota(jnp.int32, window.shape, 1)
        earlier = jnp.where(lane == 0, 0.0, pltpu.roll(window, 1, 1))
        later = jnp.where(lane == 255, 0.0, pltpu.roll(window, 255, 1))
        for dr, value in enumerate((earlier, window, later)):
            x[:, dr * 48 : dr * 48 + 48, :] = value.astype(BF).reshape(7, 48, 256)

    a2a = s.a2a_sem

    load.rtab_inv.wait()
    load.stab_inv.wait()
    load.kspace.wait()
    to_send(s.stage.kspace, s.send_one, True)
    pl.semaphore_wait(barrier, 49)
    exchange(s.send_one, s.recv_one, a2a.at[0], a2a.at[1], 1, 32)
    s.recv_one[slab] = s.send_one[slab]

    load.cotangent.wait()
    to_send(s.stage.cotangent, s.send_two, False)
    s.recv_two[slab] = s.send_two[slab]
    exchange(s.send_two, s.recv_two, a2a.at[2], a2a.at[3], 1, 32)

    load.band.wait()
    load.pick_one.wait()
    load.pick_back.wait()
    load.pick_two.wait()
    band = s.stage.band[...]
    row_pick = s.row_pick[...]
    s.taps[...] = jnp.zeros((128, 128), F32)
    for at in range(27):
        ds, dp, dr = at // 9, at // 3 % 3, at % 3
        s.taps[2 * at : 2 * at + 2, 0:CH] = s.conv_one[ds, dp, dr].astype(F32)
        s.taps[54 + 2 * at : 56 + 2 * at, 0:CH] = s.conv_two[ds, dp, dr].astype(F32)
    taps = s.taps[...].astype(BF)
    taps_t = s.taps[...].T.astype(BF)

    def banded(picks):
        total = jnp.zeros((432, 512), F32)
        for dp in range(3):
            tall = dot(row_pick, dot(taps_t, picks[dp]).astype(BF))
            total = total + jnp.where(band.astype(F32) == dp, tall, 0.0)
        return total.astype(BF)

    s.w_one[...] = banded(s.stage.pick_one)
    s.w_back[...] = banded(s.stage.pick_back)
    band_two = s.band_two[...]
    wide = dot(taps, s.col_pick_two[...]).astype(BF)
    for ds in range(3):
        total = jnp.zeros((96, 512), F32)
        for dp in range(3):
            tall = dot(s.stage.pick_two[ds * 3 + dp], wide)
            total = total + jnp.where(band_two.astype(F32) == dp, tall, 0.0)
        s.w_two[ds] = total.astype(BF)
    column = lax.broadcasted_iota(jnp.int32, (432, 128), 1)
    extra = blank(432, 128)
    row_b = lax.broadcasted_iota(jnp.int32, (128, 128), 0)
    bias = jnp.zeros((128, 128), F32)
    for at in range(CH):
        bias = jnp.where(row_b == at, s.bias_one[at], bias)
    for at, piece in enumerate(thirds(bias)):
        extra = jnp.where(column == 48 + at, dot(row_pick, piece), extra.astype(F32)).astype(BF)
    s.w_one[:, 384:512] = jnp.where(column >= 48, extra, s.w_one[:, 384:512])

    load.measured.wait()
    for part in range(2):
        for c in range(2):
            low, high = to_rows(s.stage.measured[part, c, :, 0], s.stage.measured[part, c, :, 1])
            s.meas_rows[0, part, c] = low
            s.meas_rows[1, part, c] = high

    exchange_arrived(s.recv_one, a2a.at[1])
    exchange_sent(s.send_one, a2a.at[0])
    load.ptab_inv.wait()
    load.maps.wait()
    rs_sem = s.rs_sem
    combine(s.recv_one, s.part_own, s.rs_send, s.rs_recv, rs_sem.at[0], rs_sem.at[1], True)
    image = combined(s.part_own, s.rs_send, s.rs_recv, rs_sem.at[0], rs_sem.at[1])
    halo = s.halo_sem
    halo_start(image, s.planes, s.edges, s.hp_recv, s.he_recv, halo.at[0])
    halo_finish(s.planes, s.hp_recv, s.he_recv, halo.at[0], s.x)

    x = s.x
    hidden = s.hidden
    row = lax.broadcasted_iota(jnp.int32, (432, 256), 0)
    inside = ((row >= 24) | (coil > 0)) & ((row < 408) | (coil < 7))
    own_rows = (row >= 24) & (row < 408)
    for plane in range(5):
        pre = dot(s.w_one[...], with_ones(x[plane : plane + 3].reshape(432, 256)))
        if 1 <= plane <= 3:
            s.pre[plane - 1] = pre
        value = pre / (1.0 + jnp.exp(-pre))
        keep = inside
        if plane == 0:
            keep = inside & (slab > 0)
        if plane == 4:
            keep = inside & (slab < 31)
        hidden[plane] = deep(jnp.where(keep, value, 0.0).astype(BF))
    lane = lax.broadcasted_iota(jnp.int32, (32, 256), 1)
    out_row = lax.broadcasted_iota(jnp.int32, (32, 256), 0)
    bias_two = jnp.where(out_row < 16, s.bias_two[0], s.bias_two[1])
    for plane in range(3):
        taps = jnp.zeros((96, 256), F32)
        for ds in range(3):
            taps = taps + dot(s.w_two[ds], hidden[plane + ds])
        earlier = jnp.where(lane == 0, 0.0, pltpu.roll(taps[0:32], 1, 1))
        later = jnp.where(lane == 255, 0.0, pltpu.roll(taps[64:96], 255, 1))
        update = earlier + taps[32:64] + later + bias_two
        s.ag_send[plane] = update.astype(BF)
    ag_sem = s.ag_sem

    @pl.loop(1, 8)
    def _(k):
        target = lax.rem(coil + k, 8)
        pltpu.make_async_remote_copy(
            src_ref=s.ag_send,
            dst_ref=s.ag_recv.at[coil],
            send_sem=ag_sem.at[0],
            recv_sem=ag_sem.at[1],
            device_id=(target, slab),
            device_id_type=MESH,
        ).start()

    s.ag_recv[coil] = s.ag_send[...]

    exchange_arrived(s.recv_two, a2a.at[3])
    exchange_sent(s.send_two, a2a.at[2])
    combine(s.recv_two, s.part_own, s.part_own, s.rs_recv_b, rs_sem.at[2], rs_sem.at[3], False)

    drained(s.ag_recv.at[pl.ds(0, 7)], ag_sem.at[1])
    drained(s.ag_recv.at[pl.ds(0, 7)], ag_sem.at[0])

    load.ptab_fwd.wait()
    for plane in range(3):
        u_real = s.ag_recv[:, plane, 0:16, :].reshape(128, 256).astype(F32)
        u_imag = s.ag_recv[:, plane, 16:32, :].reshape(128, 256).astype(F32)
        parts = []
        for c in range(2):
            m_real, m_imag = s.stage.maps[0, c, plane], s.stage.maps[1, c, plane]
            parts.append(m_real * u_real - m_imag * u_imag)
            parts.append(m_real * u_imag + m_imag * u_real)
        e_high, e_low = split(jnp.concatenate(parts, axis=0))
        out = dot(s.stage.ptab_fwd[...], jnp.concatenate([e_high, e_low, e_high], axis=0))
        s.send_three[:, plane * 16 : plane * 16 + 16, :] = out.astype(BF).reshape(32, 16, 256)
    exchange(s.send_three, s.recv_three, a2a.at[4], a2a.at[5], 1, 32)
    s.recv_three[slab] = s.send_three[slab]

    field = combined(s.part_own, s.part_own, s.rs_recv_b, rs_sem.at[2], rs_sem.at[3])
    halo_start(field, s.planes_b, s.edges_b, s.hp_recv_b, s.he_recv_b, halo.at[1])
    halo_finish(s.planes_b, s.hp_recv_b, s.he_recv_b, halo.at[1], s.xg)
    xg = s.xg
    band = s.stage.band[...]
    grad_one = jnp.zeros((432, 512), F32)
    grad_two = jnp.zeros((432, 512), F32)
    back_sum = jnp.zeros((432, 256), F32)
    for plane in range(3):
        near = deep(xg[plane + 1 : plane + 4].reshape(432, 256))
        back_hidden = dot(s.w_back[...], near)
        pre = s.pre[plane]
        sigmoid = 1.0 / (1.0 + jnp.exp(-pre))
        back = back_hidden * sigmoid * (1.0 + pre * (1.0 - sigmoid))
        back = jnp.where(own_rows, back, 0.0)
        back_sum = back_sum + back
        grad_one = grad_one + dot_rows(
            back.astype(BF), deep(x[plane + 1 : plane + 4].reshape(432, 256))
        )
        mine = jnp.where(own_rows, hidden[plane + 1, :432], blank(432))
        grad_two = grad_two + dot_rows(mine, near)
    row_pick_t = s.row_pick_t[...]
    col_pick_t = s.col_pick_t[...]
    pack = jnp.zeros((32, 128), F32)
    for first, grad in ((0, grad_one), (54, grad_two)):
        pieces = split(grad)
        for dp in range(3):
            on_band = band == dp
            left = jnp.zeros((32, 512), F32)
            for piece in pieces:
                left = left + dot(row_pick_t, deep(jnp.where(on_band, piece, blank(432, 512))))
            piece = pick_cols(left, col_pick_t)
            at = first + 18 * dp
            pack = pack + (pltpu.roll(piece, at, 1) if at else piece)
    lane_p = lax.broadcasted_iota(jnp.int32, (32, 128), 1)
    row_p = lax.broadcasted_iota(jnp.int32, (32, 128), 0)
    bias_grad = sum(dot(row_pick_t, deep(piece)) for piece in split(back_sum))
    bias_grad = jnp.sum(bias_grad, axis=1, keepdims=True)
    pack = pack + jnp.where(lane_p == 108, bias_grad, 0.0)
    real_sum = jnp.sum(field[:, 0])
    imag_sum = jnp.sum(field[:, 1])
    pack = pack + jnp.where(
        lane_p == 109, jnp.where(row_p == 0, real_sum, jnp.where(row_p == 1, imag_sum, 0.0)), 0.0
    )
    sum_send, sum_sem = s.sum_send, s.sum_sem
    sum_send[0] = pack[:24]

    def spread_start(stage, recv, size, mine, target_of):
        recv[mine] = sum_send[stage]

        @pl.loop(1, size)
        def _(k):
            pltpu.make_async_remote_copy(
                src_ref=sum_send.at[stage],
                dst_ref=recv.at[mine],
                send_sem=sum_sem.at[2 * stage],
                recv_sem=sum_sem.at[2 * stage + 1],
                device_id=target_of(k),
                device_id_type=MESH,
            ).start()

    def spread_end(stage, recv, size):
        drained(recv.at[pl.ds(0, size - 1)], sum_sem.at[2 * stage + 1])
        drained(recv.at[pl.ds(0, size - 1)], sum_sem.at[2 * stage])

    def added(recv, size):
        total = recv[0]
        for k in range(1, size):
            total = total + recv[k]
        return total

    core = lax.rem(slab, 2)
    place_one = coil * 2 + core

    def target_one(k):
        to = lax.rem(place_one + k, 16)
        return lax.div(to, 2), slab - core + lax.rem(to, 2)

    spread_start(0, s.sum_near, 16, place_one, target_one)
    spread_end(0, s.sum_near, 16)
    sum_send[1] = added(s.sum_near, 16)
    spread_start(1, s.sum_far, 16, lax.div(slab, 2), lambda k: (coil, lax.rem(slab + 2 * k, 32)))

    load.rtab_fwd.wait()
    load.stab_fwd.wait()
    step = s.step[0]
    row_o = lax.broadcasted_iota(jnp.int32, (192, 128), 0)
    col_o = lax.broadcasted_iota(jnp.int32, (192, 128), 1)
    slice_o = jnp.where(row_o >= 96, row_o - 96, row_o)
    col_imag = ((col_o >= 24) & (col_o < 48)) | (col_o >= 72)
    col_l = lax.broadcasted_iota(jnp.int32, (8, 128), 1)
    line_l = jnp.full((8, 128), -1, jnp.int32)
    for at in range(LINES):
        here = (col_l == at) | (col_l == at + 24) | (col_l == at + 48) | (col_l == at + 72)
        line_l = jnp.where(here, s.lines[at], line_l)
    picked = (slice_o == line_l[0:1]) & ((row_o >= 96) == col_imag)
    place = jnp.where(picked, 1.0, 0.0)
    keep = 1.0 - step * 0.5 * jnp.sum(place, axis=1, keepdims=True)
    place = place.astype(BF)
    exchange_arrived(s.recv_three, a2a.at[5])
    exchange_sent(s.send_three, a2a.at[4])
    z, y = s.z, s.y
    first = low_half((48, 8, 256), 1)
    for chunk in range(4):
        values = s.recv_three[chunk * 8 : chunk * 8 + 8].reshape(384, 256)
        uv = dot(jnp.concatenate([values, values], axis=1), s.stage.rtab_fwd[...])
        u = uv[:, :256].reshape(48, 8, 256)
        v = pltpu.roll(uv[:, 256:].reshape(48, 8, 256), 4, 1)
        full = (u + jnp.where(first, -v, v)).reshape(384, 256)
        y[0, chunk * 384 : chunk * 384 + 384, :] = full[:, :128]
        y[1, chunk * 384 : chunk * 384 + 384, :] = full[:, 128:]
    for c in range(2):
        for p in range(4):
            parts, lines, held = [], [], []
            for part in range(2):
                pick = pl.ds(c * 8 + part * 4 + p, 96, stride=16)
                parts.append(jnp.concatenate([y[0, pick, :], y[1, pick, :]], axis=1))
                pick = pl.ds(p, 24, stride=4)
                lines.append(
                    jnp.concatenate(
                        [s.meas_rows[half, part, c, pick, :] for half in range(2)], axis=1
                    )
                )
                pick = pl.ds(p, 96, stride=4)
                held.append(
                    jnp.concatenate(
                        [s.rows[half, part, c, pick, :] for half in range(2)], axis=1
                    )
                )
            z_high, z_low = split(jnp.concatenate(parts, axis=0))
            out = dot(s.stage.stab_fwd[...], deep(jnp.concatenate([z_high, z_low, z_high], axis=0), 640))
            m_high, m_low = split(step * jnp.concatenate(lines, axis=0))
            out = out + dot(place, jnp.concatenate([m_high, m_low, blank(32)], axis=0))
            out = out + keep * jnp.concatenate(held, axis=0)
            pick = pl.ds(p, 96, stride=4)
            for part in range(2):
                for half in range(2):
                    z[half, part, c, pick, :] = out[
                        part * 96 : part * 96 + 96, half * 128 : half * 128 + 128
                    ]
        for part in range(2):
            even, odd = from_rows(z[0, part, c], z[1, part, c])
            out_ref[part, c, :, 0] = even
            out_ref[part, c, :, 1] = odd

    spread_end(1, s.sum_far, 16)
    total = jnp.concatenate([added(s.sum_far, 16), jnp.zeros((104, 128), F32)], axis=0)
    s.taps[...] = total.T
    for at in range(27):
        ds, dp, dr = at // 9, at // 3 % 3, at % 3
        row = dp * 18 + (ds * 3 + dr) * 2
        one_ref[ds, dp, dr] = s.taps[row : row + 2, 0:CH]
        two_ref[2 - ds, 2 - dp, 2 - dr] = s.taps[54 + row : 56 + row, 0:CH]
    bias_one_ref[...] = s.taps[108:109, 0:CH]
    bias_two_ref[...] = s.taps[109:110, 0:2]


def tiles(values):
    count = values.shape[2]
    split_lanes = values.reshape(2, 2, count, 4, 2, 128).transpose(0, 1, 2, 4, 3, 5)
    return split_lanes.reshape(2, 2, count // 2, 2, 8, 128)


def untiles(values):
    split_lanes = values.reshape(2, 2, 96, 2, 4, 128).transpose(0, 1, 2, 4, 3, 5)
    return split_lanes.reshape(2, 2, 96, 4, 256)


def body(kspace, measured, sampled_lines, coil_maps, step_size, conv_one, bias_one, conv_two,
         bias_two, cotangent):
    staged_tables, direct_tables = constants()
    staged = dict(
        rtab_inv=staged_tables.pop("rtab_inv"),
        kspace=tiles(kspace),
        stab_inv=staged_tables.pop("stab_inv"),
        cotangent=tiles(cotangent),
        measured=tiles(measured),
        maps=coil_maps,
        **staged_tables,
    )
    direct = dict(
        conv_one=conv_one.transpose(0, 1, 2, 4, 3),
        conv_two=conv_two,
        **direct_tables,
    )
    scalars = dict(step=step_size, bias_two=bias_two, bias_one=bias_one, lines=sampled_lines)
    spectra = pltpu.VMEM((32, 48, 256), BF)
    parts = pltpu.VMEM((8, 3, 2, 16, 256), BF)
    planes = pltpu.VMEM((3, 32, 256), BF)
    edges = pltpu.VMEM((2, 16, 256), BF)
    hp_recv = pltpu.VMEM((2, 2, 32, 256), BF)
    he_recv = pltpu.VMEM((3, 2, 16, 256), BF)
    scratch = dict(
        load_sem=pltpu.SemaphoreType.DMA((len(staged),)),
        rows=pltpu.VMEM((2, 2, 2, 384, 128), F32),
        meas_rows=pltpu.VMEM((2, 2, 2, 96, 128), F32),
        z=pltpu.VMEM((2, 2, 2, 384, 128), F32),
        y=pltpu.VMEM((2, 1536, 128), F32),
        a2a_sem=pltpu.SemaphoreType.DMA((6,)),
        part_own=pltpu.VMEM((8, 3, 2, 16, 256), F32),
        rs_sem=pltpu.SemaphoreType.DMA((4,)),
        x=pltpu.VMEM((7, 144, 256), BF),
        xg=pltpu.VMEM((7, 144, 256), BF),
        halo_sem=pltpu.SemaphoreType.DMA((2, 4)),
        taps=pltpu.VMEM((128, 128), F32),
        w_one=pltpu.VMEM((432, 512), BF),
        w_back=pltpu.VMEM((432, 512), BF),
        w_two=pltpu.VMEM((3, 96, 512), BF),
        hidden=pltpu.VMEM((5, 512, 256), BF),
        pre=pltpu.VMEM((3, 432, 256), F32),
        ag_send=pltpu.VMEM((3, 32, 256), BF),
        ag_recv=pltpu.VMEM((8, 3, 32, 256), BF),
        ag_sem=pltpu.SemaphoreType.DMA((2,)),
        sum_send=pltpu.VMEM((2, 24, 128), F32),
        sum_near=pltpu.VMEM((16, 24, 128), F32),
        sum_far=pltpu.VMEM((16, 24, 128), F32),
        sum_sem=pltpu.SemaphoreType.DMA((4,)),
        send_one=spectra,
        send_two=spectra,
        send_three=spectra,
        recv_one=spectra,
        recv_two=spectra,
        recv_three=spectra,
        rs_send=parts,
        rs_recv=parts,
        rs_recv_b=pltpu.VMEM((8, 3, 2, 16, 256), F32),
        planes=planes,
        planes_b=planes,
        edges=edges,
        edges_b=edges,
        hp_recv=hp_recv,
        hp_recv_b=hp_recv,
        he_recv=he_recv,
        he_recv_b=he_recv,
    )
    stage = [pltpu.VMEM(value.shape, value.dtype) for value in staged.values()]

    def entry(*refs):
        refs = list(refs)

        def take(table):
            return {key: refs.pop(0) for key in table}

        h = SimpleNamespace(**take(staged))
        own = take(direct)
        own.update(take(scalars))
        outs = [refs.pop(0) for _ in range(5)]
        own.update(take(scratch))
        kernel(h, SimpleNamespace(**own, stage=SimpleNamespace(**take(staged))), *outs)

    in_vmem = pl.BlockSpec(memory_space=pltpu.VMEM)
    out, grad_one, grad_bias_one, grad_two, grad_bias_two = pl.pallas_call(
        entry,
        out_shape=(
            jax.ShapeDtypeStruct((2, 2, 48, 2, 8, 128), F32),
            jax.ShapeDtypeStruct((3, 3, 3, 2, CH), F32),
            jax.ShapeDtypeStruct((1, CH), F32),
            jax.ShapeDtypeStruct((3, 3, 3, 2, CH), F32),
            jax.ShapeDtypeStruct((1, 2), F32),
        ),
        in_specs=[pl.BlockSpec(memory_space=pl.ANY)] * len(staged)
        + [in_vmem] * len(direct)
        + [pl.BlockSpec(memory_space=pltpu.SMEM)] * len(scalars),
        out_specs=(in_vmem,) * 5,
        scratch_shapes=list(scratch.values()) + stage,
        compiler_params=pltpu.CompilerParams(
            collective_id=0, has_side_effects=True, vmem_limit_bytes=56 * 1024 * 1024
        ),
        name="cascade",
    )(*staged.values(), *direct.values(), *scalars.values())

    return (
        untiles(out),
        grad_one.transpose(0, 1, 2, 4, 3),
        grad_bias_one.reshape(CH),
        grad_two,
        grad_bias_two.reshape(2),
    )


def solution(mesh):
    kspace = P(None, "coils", None, "slabs", None)
    placed = (
        kspace,
        kspace,
        P(),
        P(None, "coils", "slabs", None, None),
        P(),
        P(),
        P(),
        P(),
        P(),
        kspace,
    )
    return jax.shard_map(
        body,
        mesh=mesh,
        in_specs=placed,
        out_specs=(kspace, P(), P(), P(), P()),
        check_vma=False,
    )
```

```python
from types import SimpleNamespace

import jax
import jax.numpy as jnp
import ml_dtypes
import numpy as np
from jax import lax
from jax.experimental import pallas as pl
from jax.experimental.pallas import tpu as pltpu
from jax.sharding import PartitionSpec as P

NS, NP, NR, CH, LINES = 96, 128, 256, 18, 24
BF, F32 = jnp.bfloat16, jnp.float32
MESH = pl.DeviceIdType.MESH


def dft(n, direction):
    index = np.arange(n)
    angles = (np.outer(index, index) % n) * (2.0 * np.pi / n)
    return np.cos(angles) / np.sqrt(n), direction * np.sin(angles) / np.sqrt(n)


def split_np(table):
    high = table.astype(ml_dtypes.bfloat16)
    low = (table - high.astype(np.float64)).astype(ml_dtypes.bfloat16)
    return high, low


def readout_table(direction, passes):
    cos, sin = dft(NR, direction)
    high, low = split_np(np.concatenate([cos, sin], axis=1))
    return np.concatenate([high, high, low] if passes == 3 else [high, low], axis=0)


def slice_table(direction):
    cos, sin = dft(NS, direction)
    high, low = split_np(np.block([[cos, -sin], [sin, cos]]))
    return np.concatenate([high, high, low, np.zeros((192, 64))], axis=1)


def phase_table(direction):
    cos, sin = dft(NP, direction)
    pair = np.array([[cos, -sin], [sin, cos]])
    full = np.zeros((2, 2, NP, 2, 2, NP))
    for c in range(2):
        full[c, :, :, c] = pair.transpose(0, 2, 1, 3)
    return full


def phase_inverse():
    full = phase_table(1.0).reshape(512, 2, 2, 32, 4)
    ordered = full.transpose(0, 3, 1, 2, 4).reshape(512, 512)
    return np.concatenate(split_np(ordered), axis=1)


def phase_forward():
    full = phase_table(-1.0).reshape(2, 2, 32, 4, 512)
    ordered = full.transpose(2, 0, 1, 3, 4).reshape(512, 512)
    high, low = split_np(ordered)
    return np.concatenate([high, high, low], axis=1)


def edge_picks():
    pick = np.zeros((2, 16, 8, 16), np.float32)
    for plane in range(6):
        for k in range(2):
            pick[0, plane * 2 + k, plane, k] = 1
            pick[1, plane * 2 + k, plane, 14 + k] = 1
    return pick.reshape(32, 128)


def window_picks(planes):
    count = len(planes)
    rows = count * 32
    pick = np.zeros((count, 2, 24, 128), np.float32)
    for i, plane in enumerate(planes):
        for part in range(2):
            for t in range(2):
                pick[i, part, t, rows + (plane * 2 + part) * 2 + t] = 1
                pick[i, part, 18 + t, rows + 16 + (plane * 2 + part) * 2 + t] = 1
            for t in range(16):
                pick[i, part, 2 + t, (i * 2 + part) * 16 + t] = 1
    return pick.reshape(count * 48, 128)


def constants():
    rows = np.arange(432)
    col_p = rows % 24
    row_p = rows // 24
    band = np.full((432, 512), -100.0)
    band[:, :432] = col_p[None, :] - row_p[:, None]
    row_pick = np.zeros((432, 128), np.float32)
    row_pick[rows, rows % 24] = 1
    row_pick_t = np.zeros((32, 512), np.float32)
    row_pick_t[rows % 24, rows] = 1
    col_pick = np.zeros((128, 512), np.float32)
    col_pick[rows // 24, rows] = 1
    out_rows = np.arange(96)
    band_two = np.full((96, 512), -100.0)
    band_two[:, :432] = row_p[None, :] - (out_rows % 16)[:, None]
    out_pair = out_rows // 16
    pick_two = np.zeros((9, 96, 128), np.float32)
    pick_one = np.zeros((3, 128, 512), np.float32)
    pick_back = np.zeros((3, 128, 512), np.float32)
    group = rows // 24
    g_ds, g_dr, g_part = group // 6, group // 2 % 3, group % 2
    for at in range(9):
        pick_two[at, out_rows, 54 + (at * 3 + out_pair // 2) * 2 + out_pair % 2] = 1
    for dp in range(3):
        pick_one[dp, (g_ds * 9 + dp * 3 + g_dr) * 2 + g_part, rows] = 1
        flipped = ((2 - g_ds) * 9 + (2 - dp) * 3 + 2 - g_dr) * 2 + g_part
        pick_back[dp, 54 + flipped, rows] = 1
    col_pick_two = np.zeros((128, 512), np.float32)
    col_pick_two[rows % 24, rows] = 1
    staged = dict(
        rtab_inv=readout_table(1.0, 3),
        stab_inv=slice_table(1.0),
        ptab_inv=phase_inverse(),
        ptab_fwd=phase_forward(),
        rtab_fwd=readout_table(-1.0, 2),
        stab_fwd=slice_table(-1.0),
        band=band,
        pick_one=pick_one,
        pick_back=pick_back,
        pick_two=pick_two,
    )
    direct = dict(
        pick_edge=edge_picks(),
        pick_prev=window_picks((1, 2)),
        pick_own=window_picks((0, 1, 2)),
        pick_next=window_picks((0, 1)),
        row_pick=row_pick,
        band_two=band_two,
        col_pick_two=col_pick_two,
        row_pick_t=row_pick_t,
        col_pick_t=col_pick.T,
    )

    def low(table):
        return {k: jnp.asarray(np.asarray(v).astype(ml_dtypes.bfloat16)) for k, v in table.items()}

    return low(staged), low(direct)


def dot(a, b):
    return lax.dot_general(a, b, (((1,), (0,)), ((), ())), preferred_element_type=F32)


def dot_rows(a, b):
    return lax.dot_general(a, b, (((1,), (1,)), ((), ())), preferred_element_type=F32)


def split(value):
    high = value.astype(BF)
    return high, (value - high.astype(F32)).astype(BF)


def thirds(value):
    high, rest = value.astype(BF), value
    rest = rest - high.astype(F32)
    middle = rest.astype(BF)
    return high, middle, (rest - middle.astype(F32)).astype(BF)


def pick_rows(pick, value):
    return sum(dot(pick, piece) for piece in thirds(value))


def pick_cols(value, pick):
    return sum(dot(piece, pick) for piece in thirds(value))


def blank(rows, lanes=256):
    return jnp.zeros((rows, lanes), BF)


def deep(value, rows=512):
    return jnp.concatenate([value, blank(rows - value.shape[0], value.shape[1])], axis=0)


def with_ones(value):
    return jnp.concatenate([value, jnp.ones((80, 256), BF)], axis=0)


def low_half(shape, axis):
    return lax.broadcasted_iota(jnp.int32, shape, axis) < 4


def to_rows(even, odd):
    first = low_half(even.shape, 1)
    low = jnp.where(first, even, pltpu.roll(odd, 4, 1))
    high = jnp.where(first, pltpu.roll(even, 4, 1), odd)
    return low.reshape(-1, 128), high.reshape(-1, 128)


def from_rows(low, high):
    low = low.reshape(-1, 8, 128)
    high = high.reshape(-1, 8, 128)
    first = low_half(low.shape, 1)
    even = jnp.where(first, low, pltpu.roll(high, 4, 1))
    odd = jnp.where(first, pltpu.roll(low, 4, 1), high)
    return even, odd


def kernel(h, s, out_ref, one_ref, bias_one_ref, two_ref, bias_two_ref):
    coil = lax.axis_index("coils")
    slab = lax.axis_index("slabs")

    load = SimpleNamespace()
    for at, (name, source) in enumerate(vars(h).items()):
        copy = pltpu.make_async_copy(source, getattr(s.stage, name), s.load_sem.at[at])
        setattr(load, name, copy)
        copy.start()

    barrier = pltpu.get_barrier_semaphore()

    def greet(target_coil, target_slab):
        pl.semaphore_signal(
            barrier, inc=1, device_id=(target_coil, target_slab), device_id_type=MESH
        )

    @pl.loop(1, 32)
    def _(k):
        greet(coil, lax.rem(slab + k, 32))

    @pl.loop(1, 8)
    def _(k):
        greet(lax.rem(coil + k, 8), slab)

    @pl.loop(1, 8)
    def _(k):
        greet(lax.rem(coil + k, 8), slab + 1 - 2 * lax.rem(slab, 2))

    for dc in (1, 7):
        for ds in (1, 31):
            greet(lax.rem(coil + dc, 8), lax.rem(slab + ds, 32))

    def to_send(v, send, keep):
        rtab = s.stage.rtab_inv[...]
        stab = s.stage.stab_inv[...]
        z, y = s.z, s.y
        for c in range(2):
            uv = []
            for part in range(2):
                low, high = to_rows(v[part, c, :, 0], v[part, c, :, 1])
                if keep:
                    s.rows[0, part, c] = low
                    s.rows[1, part, c] = high
                x_high, x_low = split(jnp.concatenate([low, high], axis=1))
                uv.append(dot(jnp.concatenate([x_high, x_low, x_high], axis=1), rtab))
            z_real = uv[0][:, :256] - uv[1][:, 256:]
            z_imag = uv[1][:, :256] + uv[0][:, 256:]
            for half in range(2):
                lanes = slice(half * 128, half * 128 + 128)
                z[half, 0, c] = z_real[:, lanes]
                z[half, 1, c] = z_imag[:, lanes]
            for p in range(4):
                pick = pl.ds(p, 96, stride=4)
                parts = [
                    jnp.concatenate([z[0, part, c, pick, :], z[1, part, c, pick, :]], axis=1)
                    for part in range(2)
                ]
                z_high, z_low = split(jnp.concatenate(parts, axis=0))
                out = dot(stab, deep(jnp.concatenate([z_high, z_low, z_high], axis=0), 640))
                for part in range(2):
                    for half in range(2):
                        y[half, pl.ds(c * 8 + part * 4 + p, 96, stride=16), :] = out[
                            part * 96 : part * 96 + 96, half * 128 : half * 128 + 128
                        ]
        full = jnp.concatenate([y[0], y[1]], axis=1).astype(BF)
        send[...] = full.reshape(32, 48, 256)

    def exchange(send, recv, send_sem, recv_sem, first, last):
        @pl.loop(first, last)
        def _(k):
            target = lax.rem(slab + lax.rem(k * 13, 32), 32)
            pltpu.make_async_remote_copy(
                src_ref=send.at[target],
                dst_ref=recv.at[slab],
                send_sem=send_sem,
                recv_sem=recv_sem,
                device_id=(coil, target),
                device_id_type=MESH,
            ).start()

    def drained(ref, sem):
        pltpu.make_async_copy(ref, ref, sem).wait()

    def exchange_sent(send, send_sem):
        drained(send.at[pl.ds(0, 31)], send_sem)

    def exchange_arrived(recv, recv_sem):
        drained(recv.at[pl.ds(0, 31)], recv_sem)

    def combine(recv, part_own, rs_send, rs_recv, send_sem, recv_sem, low):
        table = s.stage.ptab_inv[...]
        maps = s.stage.maps
        for plane in range(3):
            values = recv[:, 16 * plane : 16 * plane + 16, :].reshape(512, 256)
            image = dot(table, jnp.concatenate([values, values], axis=0))
            real = jnp.zeros((128, 256), F32)
            imag = jnp.zeros((128, 256), F32)
            for c in range(2):
                m_real, m_imag = maps[0, c, plane], maps[1, c, plane]
                i_real = image[c * 256 : c * 256 + 128]
                i_imag = image[c * 256 + 128 : c * 256 + 256]
                real = real + m_real * i_real + m_imag * i_imag
                imag = imag + m_real * i_imag - m_imag * i_real
            part_own[:, plane, 0] = real.reshape(8, 16, 256)
            part_own[:, plane, 1] = imag.reshape(8, 16, 256)
            if low:
                rs_send[:, plane, 0] = real.astype(BF).reshape(8, 16, 256)
                rs_send[:, plane, 1] = imag.astype(BF).reshape(8, 16, 256)

        @pl.loop(1, 8)
        def _(k):
            target = lax.rem(coil + k, 8)
            pltpu.make_async_remote_copy(
                src_ref=rs_send.at[target],
                dst_ref=rs_recv.at[coil],
                send_sem=send_sem,
                recv_sem=recv_sem,
                device_id=(target, slab),
                device_id_type=MESH,
            ).start()

        rs_recv[coil] = jnp.zeros((3, 2, 16, 256), rs_recv.dtype)

    def combined(part_own, rs_send, rs_recv, send_sem, recv_sem):
        drained(rs_recv.at[pl.ds(0, 7)], recv_sem)
        drained(rs_send.at[pl.ds(0, 7)], send_sem)
        total = part_own[coil]
        for k in range(8):
            total = total + rs_recv[k].astype(F32)
        return total

    def halo_start(field, planes, edges, hp_recv, he_recv, sems):
        planes[...] = field.astype(BF).reshape(3, 32, 256)
        picked = dot(s.pick_edge[...], deep(planes[...].reshape(96, 256), 128))
        edges[...] = picked.astype(BF).reshape(2, 16, 256)
        prev, after = lax.rem(slab + 31, 32), lax.rem(slab + 1, 32)

        def send(src, dst, pair, target):
            pltpu.make_async_remote_copy(
                src_ref=src, dst_ref=dst, send_sem=sems.at[pair], recv_sem=sems.at[pair + 1],
                device_id=target, device_id_type=MESH,
            ).start()

        send(planes.at[pl.ds(1, 2)], hp_recv.at[0], 0, (coil, after))
        send(planes.at[pl.ds(0, 2)], hp_recv.at[1], 0, (coil, prev))
        for at, target_slab in ((2, prev), (1, slab), (0, after)):
            send(edges.at[1], he_recv.at[at, 0], 2, (lax.rem(coil + 1, 8), target_slab))
            send(edges.at[0], he_recv.at[at, 1], 2, (lax.rem(coil + 7, 8), target_slab))

    def halo_finish(planes, hp_recv, he_recv, sems, x):
        drained(hp_recv, sems.at[1])
        drained(he_recv, sems.at[3])
        drained(hp_recv, sems.at[0])
        drained(he_recv, sems.at[2])
        zero_edge = jnp.zeros((16, 256), BF)

        def group(body, at):
            lower = jnp.where(coil > 0, he_recv[at, 0], zero_edge)
            upper = jnp.where(coil < 7, he_recv[at, 1], zero_edge)
            return jnp.concatenate([body, lower, upper], axis=0)

        before = group(hp_recv[0].reshape(64, 256), 0)
        own = group(planes[...].reshape(96, 256), 1)
        after = group(hp_recv[1].reshape(64, 256), 2)
        before = dot(s.pick_prev[...], deep(before, 128))
        after = dot(s.pick_next[...], deep(after, 128))
        before = jnp.where(slab > 0, before, jnp.zeros_like(before))
        after = jnp.where(slab < 31, after, jnp.zeros_like(after))
        window = jnp.concatenate([before, dot(s.pick_own[...], own), after], axis=0)
        lane = lax.broadcasted_iota(jnp.int32, window.shape, 1)
        earlier = jnp.where(lane == 0, 0.0, pltpu.roll(window, 1, 1))
        later = jnp.where(lane == 255, 0.0, pltpu.roll(window, 255, 1))
        for dr, value in enumerate((earlier, window, later)):
            x[:, dr * 48 : dr * 48 + 48, :] = value.astype(BF).reshape(7, 48, 256)

    a2a = s.a2a_sem

    load.rtab_inv.wait()
    load.stab_inv.wait()
    load.kspace.wait()
    to_send(s.stage.kspace, s.send_one, True)
    pl.semaphore_wait(barrier, 49)
    exchange(s.send_one, s.recv_one, a2a.at[0], a2a.at[1], 1, 32)
    s.recv_one[slab] = s.send_one[slab]

    load.cotangent.wait()
    to_send(s.stage.cotangent, s.send_two, False)
    s.recv_two[slab] = s.send_two[slab]
    exchange(s.send_two, s.recv_two, a2a.at[2], a2a.at[3], 1, 32)

    load.band.wait()
    load.pick_one.wait()
    load.pick_back.wait()
    load.pick_two.wait()
    band = s.stage.band[...]
    row_pick = s.row_pick[...]
    s.taps[...] = jnp.zeros((128, 128), F32)
    for at in range(27):
        ds, dp, dr = at // 9, at // 3 % 3, at % 3
        s.taps[2 * at : 2 * at + 2, 0:CH] = s.conv_one[ds, dp, dr].astype(F32)
        s.taps[54 + 2 * at : 56 + 2 * at, 0:CH] = s.conv_two[ds, dp, dr].astype(F32)
    taps = s.taps[...].astype(BF)
    taps_t = s.taps[...].T.astype(BF)

    def banded(picks):
        total = jnp.zeros((432, 512), F32)
        for dp in range(3):
            tall = dot(row_pick, dot(taps_t, picks[dp]).astype(BF))
            total = total + jnp.where(band.astype(F32) == dp, tall, 0.0)
        return total.astype(BF)

    s.w_one[...] = banded(s.stage.pick_one)
    s.w_back[...] = banded(s.stage.pick_back)
    band_two = s.band_two[...]
    wide = dot(taps, s.col_pick_two[...]).astype(BF)
    for ds in range(3):
        total = jnp.zeros((96, 512), F32)
        for dp in range(3):
            tall = dot(s.stage.pick_two[ds * 3 + dp], wide)
            total = total + jnp.where(band_two.astype(F32) == dp, tall, 0.0)
        s.w_two[ds] = total.astype(BF)
    column = lax.broadcasted_iota(jnp.int32, (432, 128), 1)
    extra = blank(432, 128)
    row_b = lax.broadcasted_iota(jnp.int32, (128, 128), 0)
    bias = jnp.zeros((128, 128), F32)
    for at in range(CH):
        bias = jnp.where(row_b == at, s.bias_one[at], bias)
    for at, piece in enumerate(thirds(bias)):
        extra = jnp.where(column == 48 + at, dot(row_pick, piece), extra.astype(F32)).astype(BF)
    s.w_one[:, 384:512] = jnp.where(column >= 48, extra, s.w_one[:, 384:512])

    load.measured.wait()
    for part in range(2):
        for c in range(2):
            low, high = to_rows(s.stage.measured[part, c, :, 0], s.stage.measured[part, c, :, 1])
            s.meas_rows[0, part, c] = low
            s.meas_rows[1, part, c] = high

    exchange_arrived(s.recv_one, a2a.at[1])
    exchange_sent(s.send_one, a2a.at[0])
    load.ptab_inv.wait()
    load.maps.wait()
    rs_sem = s.rs_sem
    combine(s.recv_one, s.part_own, s.rs_send, s.rs_recv, rs_sem.at[0], rs_sem.at[1], True)
    image = combined(s.part_own, s.rs_send, s.rs_recv, rs_sem.at[0], rs_sem.at[1])
    halo = s.halo_sem
    halo_start(image, s.planes, s.edges, s.hp_recv, s.he_recv, halo.at[0])
    exchange_arrived(s.recv_two, a2a.at[3])
    exchange_sent(s.send_two, a2a.at[2])
    combine(s.recv_two, s.part_own, s.part_own, s.rs_recv_b, rs_sem.at[2], rs_sem.at[3], False)

    halo_finish(s.planes, s.hp_recv, s.he_recv, halo.at[0], s.x)

    x = s.x
    hidden = s.hidden
    row = lax.broadcasted_iota(jnp.int32, (432, 256), 0)
    inside = ((row >= 24) | (coil > 0)) & ((row < 408) | (coil < 7))
    own_rows = (row >= 24) & (row < 408)
    for plane in range(5):
        pre = dot(s.w_one[...], with_ones(x[plane : plane + 3].reshape(432, 256)))
        if 1 <= plane <= 3:
            s.pre[plane - 1] = pre
        value = pre / (1.0 + jnp.exp(-pre))
        keep = inside
        if plane == 0:
            keep = inside & (slab > 0)
        if plane == 4:
            keep = inside & (slab < 31)
        hidden[plane] = deep(jnp.where(keep, value, 0.0).astype(BF))
    lane = lax.broadcasted_iota(jnp.int32, (32, 256), 1)
    out_row = lax.broadcasted_iota(jnp.int32, (32, 256), 0)
    bias_two = jnp.where(out_row < 16, s.bias_two[0], s.bias_two[1])
    for plane in range(3):
        taps = jnp.zeros((96, 256), F32)
        for ds in range(3):
            taps = taps + dot(s.w_two[ds], hidden[plane + ds])
        earlier = jnp.where(lane == 0, 0.0, pltpu.roll(taps[0:32], 1, 1))
        later = jnp.where(lane == 255, 0.0, pltpu.roll(taps[64:96], 255, 1))
        update = earlier + taps[32:64] + later + bias_two
        s.ag_send[plane] = update.astype(BF)
    ag_sem = s.ag_sem

    @pl.loop(1, 8)
    def _(k):
        target = lax.rem(coil + k, 8)
        pltpu.make_async_remote_copy(
            src_ref=s.ag_send,
            dst_ref=s.ag_recv.at[coil],
            send_sem=ag_sem.at[0],
            recv_sem=ag_sem.at[1],
            device_id=(target, slab),
            device_id_type=MESH,
        ).start()

    s.ag_recv[coil] = s.ag_send[...]

    drained(s.ag_recv.at[pl.ds(0, 7)], ag_sem.at[1])
    drained(s.ag_recv.at[pl.ds(0, 7)], ag_sem.at[0])

    load.ptab_fwd.wait()
    for plane in range(3):
        u_real = s.ag_recv[:, plane, 0:16, :].reshape(128, 256).astype(F32)
        u_imag = s.ag_recv[:, plane, 16:32, :].reshape(128, 256).astype(F32)
        parts = []
        for c in range(2):
            m_real, m_imag = s.stage.maps[0, c, plane], s.stage.maps[1, c, plane]
            parts.append(m_real * u_real - m_imag * u_imag)
            parts.append(m_real * u_imag + m_imag * u_real)
        e_high, e_low = split(jnp.concatenate(parts, axis=0))
        out = dot(s.stage.ptab_fwd[...], jnp.concatenate([e_high, e_low, e_high], axis=0))
        s.send_three[:, plane * 16 : plane * 16 + 16, :] = out.astype(BF).reshape(32, 16, 256)
    field = combined(s.part_own, s.part_own, s.rs_recv_b, rs_sem.at[2], rs_sem.at[3])
    halo_start(field, s.planes_b, s.edges_b, s.hp_recv_b, s.he_recv_b, halo.at[1])
    exchange(s.send_three, s.recv_three, a2a.at[4], a2a.at[5], 1, 32)
    s.recv_three[slab] = s.send_three[slab]

    halo_finish(s.planes_b, s.hp_recv_b, s.he_recv_b, halo.at[1], s.xg)
    xg = s.xg
    band = s.stage.band[...]
    grad_one = jnp.zeros((432, 512), F32)
    grad_two = jnp.zeros((432, 512), F32)
    back_sum = jnp.zeros((432, 256), F32)
    for plane in range(3):
        near = deep(xg[plane + 1 : plane + 4].reshape(432, 256))
        back_hidden = dot(s.w_back[...], near)
        pre = s.pre[plane]
        sigmoid = 1.0 / (1.0 + jnp.exp(-pre))
        back = back_hidden * sigmoid * (1.0 + pre * (1.0 - sigmoid))
        back = jnp.where(own_rows, back, 0.0)
        back_sum = back_sum + back
        grad_one = grad_one + dot_rows(
            back.astype(BF), deep(x[plane + 1 : plane + 4].reshape(432, 256))
        )
        mine = jnp.where(own_rows, hidden[plane + 1, :432], blank(432))
        grad_two = grad_two + dot_rows(mine, near)
    row_pick_t = s.row_pick_t[...]
    col_pick_t = s.col_pick_t[...]
    pack = jnp.zeros((32, 128), F32)
    for first, grad in ((0, grad_one), (54, grad_two)):
        pieces = split(grad)
        for dp in range(3):
            on_band = band == dp
            left = jnp.zeros((32, 512), F32)
            for piece in pieces:
                left = left + dot(row_pick_t, deep(jnp.where(on_band, piece, blank(432, 512))))
            piece = pick_cols(left, col_pick_t)
            at = first + 18 * dp
            pack = pack + (pltpu.roll(piece, at, 1) if at else piece)
    lane_p = lax.broadcasted_iota(jnp.int32, (32, 128), 1)
    row_p = lax.broadcasted_iota(jnp.int32, (32, 128), 0)
    bias_grad = sum(dot(row_pick_t, deep(piece)) for piece in split(back_sum))
    bias_grad = jnp.sum(bias_grad, axis=1, keepdims=True)
    pack = pack + jnp.where(lane_p == 108, bias_grad, 0.0)
    real_sum = jnp.sum(field[:, 0])
    imag_sum = jnp.sum(field[:, 1])
    pack = pack + jnp.where(
        lane_p == 109, jnp.where(row_p == 0, real_sum, jnp.where(row_p == 1, imag_sum, 0.0)), 0.0
    )
    sum_send, sum_sem = s.sum_send, s.sum_sem
    sum_send[0] = pack[:24]

    def spread_start(stage, recv, size, mine, target_of):
        recv[mine] = sum_send[stage]

        @pl.loop(1, size)
        def _(k):
            pltpu.make_async_remote_copy(
                src_ref=sum_send.at[stage],
                dst_ref=recv.at[mine],
                send_sem=sum_sem.at[2 * stage],
                recv_sem=sum_sem.at[2 * stage + 1],
                device_id=target_of(k),
                device_id_type=MESH,
            ).start()

    def spread_end(stage, recv, size):
        drained(recv.at[pl.ds(0, size - 1)], sum_sem.at[2 * stage + 1])
        drained(recv.at[pl.ds(0, size - 1)], sum_sem.at[2 * stage])

    def added(recv, size):
        total = recv[0]
        for k in range(1, size):
            total = total + recv[k]
        return total

    core = lax.rem(slab, 2)
    place_one = coil * 2 + core

    def target_one(k):
        to = lax.rem(place_one + k, 16)
        return lax.div(to, 2), slab - core + lax.rem(to, 2)

    spread_start(0, s.sum_near, 16, place_one, target_one)
    spread_end(0, s.sum_near, 16)
    sum_send[1] = added(s.sum_near, 16)
    spread_start(1, s.sum_far, 16, lax.div(slab, 2), lambda k: (coil, lax.rem(slab + 2 * k, 32)))

    load.rtab_fwd.wait()
    load.stab_fwd.wait()
    step = s.step[0]
    row_o = lax.broadcasted_iota(jnp.int32, (192, 128), 0)
    col_o = lax.broadcasted_iota(jnp.int32, (192, 128), 1)
    slice_o = jnp.where(row_o >= 96, row_o - 96, row_o)
    col_imag = ((col_o >= 24) & (col_o < 48)) | (col_o >= 72)
    col_l = lax.broadcasted_iota(jnp.int32, (8, 128), 1)
    line_l = jnp.full((8, 128), -1, jnp.int32)
    for at in range(LINES):
        here = (col_l == at) | (col_l == at + 24) | (col_l == at + 48) | (col_l == at + 72)
        line_l = jnp.where(here, s.lines[at], line_l)
    picked = (slice_o == line_l[0:1]) & ((row_o >= 96) == col_imag)
    place = jnp.where(picked, 1.0, 0.0)
    keep = 1.0 - step * 0.5 * jnp.sum(place, axis=1, keepdims=True)
    place = place.astype(BF)
    exchange_arrived(s.recv_three, a2a.at[5])
    exchange_sent(s.send_three, a2a.at[4])
    z, y = s.z, s.y
    first = low_half((48, 8, 256), 1)
    for chunk in range(4):
        values = s.recv_three[chunk * 8 : chunk * 8 + 8].reshape(384, 256)
        uv = dot(jnp.concatenate([values, values], axis=1), s.stage.rtab_fwd[...])
        u = uv[:, :256].reshape(48, 8, 256)
        v = pltpu.roll(uv[:, 256:].reshape(48, 8, 256), 4, 1)
        full = (u + jnp.where(first, -v, v)).reshape(384, 256)
        y[0, chunk * 384 : chunk * 384 + 384, :] = full[:, :128]
        y[1, chunk * 384 : chunk * 384 + 384, :] = full[:, 128:]
    for c in range(2):
        for p in range(4):
            parts, lines, held = [], [], []
            for part in range(2):
                pick = pl.ds(c * 8 + part * 4 + p, 96, stride=16)
                parts.append(jnp.concatenate([y[0, pick, :], y[1, pick, :]], axis=1))
                pick = pl.ds(p, 24, stride=4)
                lines.append(
                    jnp.concatenate(
                        [s.meas_rows[half, part, c, pick, :] for half in range(2)], axis=1
                    )
                )
                pick = pl.ds(p, 96, stride=4)
                held.append(
                    jnp.concatenate(
                        [s.rows[half, part, c, pick, :] for half in range(2)], axis=1
                    )
                )
            z_high, z_low = split(jnp.concatenate(parts, axis=0))
            out = dot(s.stage.stab_fwd[...], deep(jnp.concatenate([z_high, z_low, z_high], axis=0), 640))
            m_high, m_low = split(step * jnp.concatenate(lines, axis=0))
            out = out + dot(place, jnp.concatenate([m_high, m_low, blank(32)], axis=0))
            out = out + keep * jnp.concatenate(held, axis=0)
            pick = pl.ds(p, 96, stride=4)
            for part in range(2):
                for half in range(2):
                    z[half, part, c, pick, :] = out[
                        part * 96 : part * 96 + 96, half * 128 : half * 128 + 128
                    ]
        for part in range(2):
            even, odd = from_rows(z[0, part, c], z[1, part, c])
            out_ref[part, c, :, 0] = even
            out_ref[part, c, :, 1] = odd

    spread_end(1, s.sum_far, 16)
    total = jnp.concatenate([added(s.sum_far, 16), jnp.zeros((104, 128), F32)], axis=0)
    s.taps[...] = total.T
    for at in range(27):
        ds, dp, dr = at // 9, at // 3 % 3, at % 3
        row = dp * 18 + (ds * 3 + dr) * 2
        one_ref[ds, dp, dr] = s.taps[row : row + 2, 0:CH]
        two_ref[2 - ds, 2 - dp, 2 - dr] = s.taps[54 + row : 56 + row, 0:CH]
    bias_one_ref[...] = s.taps[108:109, 0:CH]
    bias_two_ref[...] = s.taps[109:110, 0:2]


def tiles(values):
    count = values.shape[2]
    split_lanes = values.reshape(2, 2, count, 4, 2, 128).transpose(0, 1, 2, 4, 3, 5)
    return split_lanes.reshape(2, 2, count // 2, 2, 8, 128)


def untiles(values):
    split_lanes = values.reshape(2, 2, 96, 2, 4, 128).transpose(0, 1, 2, 4, 3, 5)
    return split_lanes.reshape(2, 2, 96, 4, 256)


def body(kspace, measured, sampled_lines, coil_maps, step_size, conv_one, bias_one, conv_two,
         bias_two, cotangent):
    staged_tables, direct_tables = constants()
    staged = dict(
        rtab_inv=staged_tables.pop("rtab_inv"),
        kspace=tiles(kspace),
        stab_inv=staged_tables.pop("stab_inv"),
        cotangent=tiles(cotangent),
        measured=tiles(measured),
        maps=coil_maps,
        **staged_tables,
    )
    direct = dict(
        conv_one=conv_one.transpose(0, 1, 2, 4, 3),
        conv_two=conv_two,
        **direct_tables,
    )
    scalars = dict(step=step_size, bias_two=bias_two, bias_one=bias_one, lines=sampled_lines)
    spectra = pltpu.VMEM((32, 48, 256), BF)
    parts = pltpu.VMEM((8, 3, 2, 16, 256), BF)
    planes = pltpu.VMEM((3, 32, 256), BF)
    edges = pltpu.VMEM((2, 16, 256), BF)
    hp_recv = pltpu.VMEM((2, 2, 32, 256), BF)
    he_recv = pltpu.VMEM((3, 2, 16, 256), BF)
    scratch = dict(
        load_sem=pltpu.SemaphoreType.DMA((len(staged),)),
        rows=pltpu.VMEM((2, 2, 2, 384, 128), F32),
        meas_rows=pltpu.VMEM((2, 2, 2, 96, 128), F32),
        z=pltpu.VMEM((2, 2, 2, 384, 128), F32),
        y=pltpu.VMEM((2, 1536, 128), F32),
        a2a_sem=pltpu.SemaphoreType.DMA((6,)),
        part_own=pltpu.VMEM((8, 3, 2, 16, 256), F32),
        rs_sem=pltpu.SemaphoreType.DMA((4,)),
        x=pltpu.VMEM((7, 144, 256), BF),
        xg=pltpu.VMEM((7, 144, 256), BF),
        halo_sem=pltpu.SemaphoreType.DMA((2, 4)),
        taps=pltpu.VMEM((128, 128), F32),
        w_one=pltpu.VMEM((432, 512), BF),
        w_back=pltpu.VMEM((432, 512), BF),
        w_two=pltpu.VMEM((3, 96, 512), BF),
        hidden=pltpu.VMEM((5, 512, 256), BF),
        pre=pltpu.VMEM((3, 432, 256), F32),
        ag_send=pltpu.VMEM((3, 32, 256), BF),
        ag_recv=pltpu.VMEM((8, 3, 32, 256), BF),
        ag_sem=pltpu.SemaphoreType.DMA((2,)),
        sum_send=pltpu.VMEM((2, 24, 128), F32),
        sum_near=pltpu.VMEM((16, 24, 128), F32),
        sum_far=pltpu.VMEM((16, 24, 128), F32),
        sum_sem=pltpu.SemaphoreType.DMA((4,)),
        send_one=spectra,
        send_two=spectra,
        send_three=spectra,
        recv_one=spectra,
        recv_two=spectra,
        recv_three=spectra,
        rs_send=parts,
        rs_recv=parts,
        rs_recv_b=pltpu.VMEM((8, 3, 2, 16, 256), F32),
        planes=planes,
        planes_b=planes,
        edges=edges,
        edges_b=edges,
        hp_recv=hp_recv,
        hp_recv_b=hp_recv,
        he_recv=he_recv,
        he_recv_b=he_recv,
    )
    stage = [pltpu.VMEM(value.shape, value.dtype) for value in staged.values()]

    def entry(*refs):
        refs = list(refs)

        def take(table):
            return {key: refs.pop(0) for key in table}

        h = SimpleNamespace(**take(staged))
        own = take(direct)
        own.update(take(scalars))
        outs = [refs.pop(0) for _ in range(5)]
        own.update(take(scratch))
        kernel(h, SimpleNamespace(**own, stage=SimpleNamespace(**take(staged))), *outs)

    in_vmem = pl.BlockSpec(memory_space=pltpu.VMEM)
    out, grad_one, grad_bias_one, grad_two, grad_bias_two = pl.pallas_call(
        entry,
        out_shape=(
            jax.ShapeDtypeStruct((2, 2, 48, 2, 8, 128), F32),
            jax.ShapeDtypeStruct((3, 3, 3, 2, CH), F32),
            jax.ShapeDtypeStruct((1, CH), F32),
            jax.ShapeDtypeStruct((3, 3, 3, 2, CH), F32),
            jax.ShapeDtypeStruct((1, 2), F32),
        ),
        in_specs=[pl.BlockSpec(memory_space=pl.ANY)] * len(staged)
        + [in_vmem] * len(direct)
        + [pl.BlockSpec(memory_space=pltpu.SMEM)] * len(scalars),
        out_specs=(in_vmem,) * 5,
        scratch_shapes=list(scratch.values()) + stage,
        compiler_params=pltpu.CompilerParams(
            collective_id=0, has_side_effects=True, vmem_limit_bytes=56 * 1024 * 1024
        ),
        name="cascade",
    )(*staged.values(), *direct.values(), *scalars.values())

    results = (out, grad_one, grad_bias_one, grad_two, grad_bias_two)

    def hand_over(*refs):
        for at in range(5):
            refs[5 + at][...] = refs[at][...]

    out, grad_one, grad_bias_one, grad_two, grad_bias_two = pl.pallas_call(
        hand_over,
        out_shape=tuple(jax.ShapeDtypeStruct(r.shape, r.dtype) for r in results),
        in_specs=[in_vmem] * 5,
        out_specs=(in_vmem,) * 5,
        name="results",
    )(*results)
    return (
        untiles(out),
        grad_one.transpose(0, 1, 2, 4, 3),
        grad_bias_one.reshape(CH),
        grad_two,
        grad_bias_two.reshape(2),
    )


def solution(mesh):
    kspace = P(None, "coils", None, "slabs", None)
    placed = (
        kspace,
        kspace,
        P(),
        P(None, "coils", "slabs", None, None),
        P(),
        P(),
        P(),
        P(),
        P(),
        kspace,
    )
    return jax.shard_map(
        body,
        mesh=mesh,
        in_specs=placed,
        out_specs=(kspace, P(), P(), P(), P()),
        check_vma=False,
    )
```
